32 devices in a mesh: groups: 2 (over x), seq: 2 (over core), tp: 8 (over z, y).
Axes of the slice: x: 2, y: 2, z: 4, core: 2. Of those that a mesh axis runs over, the one named last changes fastest.
Arguments:
- loaded: bfloat16 [3072, 4096], P(('groups', 'seq'), 'tp'), parts along dimension 0, may hold values from -6 to 6
- block_counts: int32 [8], P(('groups', 'seq')), parts along dimension 0, may hold values from 1 to 3, 8 in all
- seq_order: int32 [16], P('groups'), parts along dimension 0, may hold values from 0 to 7, each once
- gate_weight: bfloat16 [4096, 14336], P(None, 'tp'), may hold values from -0.09375 to 0.09375
- up_weight: bfloat16 [4096, 14336], P(None, 'tp'), may hold values from -0.09375 to 0.09375
- down_weight: bfloat16 [14336, 4096], P('tp'), may hold values from -0.0625 to 0.0625
Outputs:
- ffn_output: bfloat16 [2048, 4096], P(('groups', 'seq'), 'tp'), parts along dimension 0
The draws below stay inside these ranges and needn't reach their ends.
There are 2 independent parts, one for each index of `groups`. The reference program is written for one: setup_inputs(seed, part) draws one part's arguments, and reference() takes and returns one part's arrays. A program takes and returns all parts, laid end to end along the dimension named above; an argument that names none is the same for every part. Nothing has to cross between parts.
Inputs may be any that keep to these rules, and one draw needn't show every extreme that they name: A loader's live blocks are its first block_counts slots; the counts sum to 8 and the largest is exactly 3. `seq_order`: each of the 8 block positions appears once.
All inputs are finite; a program needn't handle non-finite values.
Results may differ from the reference program's by a relative error of at most 0.013.
Values may be sent and summed in bfloat16 or wider, within the bound.
No kernel may reach another device: no remote copies, remote signals or barrier semaphores. Data moves between devices by JAX's collectives and lax.ppermute only.
A program may use at most 128 MiB of HBM per device.

```python
import math
import jax
import jax.numpy as jnp
import numpy as np
from jax import lax

D = 4096
FF = 14336
BLOCK = 128
CAP = 3
LOADERS = 4
BLOCKS = 8
TOKENS = 1024
HID_DEV = 1792


def strengthened(entries, own_key, source, target, blocks, factor):
    owner, partner = [(jnp.arange(entries.shape[axis_at]) // (entries.shape[axis_at] // blocks)).reshape([-1 if axis == axis_at else 1 for axis in range(entries.ndim)]) for axis_at in (source, target)]
    chosen = jax.random.permutation(own_key, blocks)[partner]
    strong = (owner == chosen) | (owner == (partner + blocks // 2) % blocks)
    return jnp.where(strong, factor * entries, entries)


def shard_levels(rng, extent, cuts, least, largest):
    def one(position, shards_of):
        heights = jax.random.uniform(jax.random.fold_in(jax.random.fold_in(rng, 6), position), (shards_of,), jnp.float32, least / len(cuts), largest / len(cuts))
        return jnp.repeat(jnp.exp(heights), extent[position] // shards_of).reshape((-1,) + (1,) * (len(extent) - position - 1))

    loudness = one(*cuts[0])
    for cut in cuts[1:]:
        loudness = loudness * one(*cut)
    return loudness


def split_up(count, total, reach, skew):
    portions = [(1 << 20) // math.isqrt(standing ** skew) + 1 for standing in range(2, count + 1)]
    surplus, given = total - reach - (count - 1), [1] * (count - 1)
    while surplus > 0:
        free = [i for i in range(count - 1) if given[i] < reach]
        whole, budget = sum([portions[i] for i in free]), surplus
        for i in free:
            more = min(reach - given[i], max(1, budget * portions[i] // whole), surplus)
            given[i] = given[i] + more
            surplus = surplus - more
    return np.array([reach] + given)


def uneven_parts(stream_key, count, total, limit, slope):
    if count == 2:
        one = jax.random.randint(stream_key, (), max(1, total - limit), min(limit, total - 1) + 1)
        return jnp.stack([one, total - one])
    lengths = jnp.asarray(split_up(count, total, limit, slope), jnp.int32)
    pairs = (count - 1) // 2
    giver, sink = lengths[1:1 + 2 * pairs:2], lengths[2:2 + 2 * pairs:2]
    slack = jnp.minimum(giver - 1, limit - sink)
    moved = jax.random.randint(jax.random.fold_in(stream_key, 1), (pairs,), 0, 1 << 20) % (slack + 1)
    lengths = lengths.at[1:1 + 2 * pairs:2].set(giver - moved).at[2:2 + 2 * pairs:2].set(sink + moved)
    return lengths[jax.random.permutation(jax.random.fold_in(stream_key, 2), count)]


def normal_values(own_key, extent, width, reach, cuts=(), held_as=jnp.bfloat16):
    values = width * jax.random.normal(own_key, extent, jnp.float32)
    if cuts:
        values = values * shard_levels(own_key, extent, cuts, -0.22, 0.18)
    return jnp.clip(values, -reach, reach).astype(held_as)


def heavy_noise(stream_key, extent, deviation, limit, cuts, heavy, kind=jnp.bfloat16):
    result = deviation * jax.random.normal(stream_key, extent, jnp.float32)
    if cuts:
        result = result * shard_levels(stream_key, extent, cuts, -0.22, 0.18)
    return jnp.clip(strengthened(result, jax.random.fold_in(stream_key, 3), *heavy), -limit, limit).astype(kind)


def setup_inputs(seed: int = 0, part: int = 0) -> dict:
    keys = jax.random.split(jax.random.key(seed), 7)
    own_keys = jax.random.split(jax.random.fold_in(keys[6], part), 7)
    return {
        "loaded": normal_values(own_keys[0], (LOADERS * CAP * BLOCK, D), 1.0, 6.0, ((0, 2), (1, 8))),
        "block_counts": uneven_parts(own_keys[1], LOADERS, BLOCKS, CAP, 0).astype(jnp.int32),
        "seq_order": jax.random.permutation(own_keys[2], BLOCKS).astype(jnp.int32),
        "gate_weight": normal_values(keys[3], (D, FF), D ** -0.5, 0.09375, ((1, 8),)),
        "up_weight": normal_values(keys[4], (D, FF), D ** -0.5, 0.09375, ((1, 8),)),
        "down_weight": heavy_noise(keys[5], (FF, D), FF ** -0.5, 0.0625, ((0, 8),), (0, 1, 8, 2.0)),
    }


def reference(loaded, block_counts, seq_order, gate_weight, up_weight, down_weight):
    slot_ids = jnp.arange(CAP, dtype=jnp.int32)
    offsets = (jnp.cumsum(block_counts) - block_counts).astype(jnp.int32)
    flat_index = offsets[:, None] + slot_ids[None, :]
    is_live = slot_ids[None, :] < block_counts[:, None]
    target = seq_order[jnp.clip(flat_index, 0, BLOCKS - 1)]
    target = jnp.where(is_live, target, BLOCKS).reshape(-1).astype(jnp.int32)
    all_blocks = loaded.reshape(LOADERS * CAP, BLOCK, D)
    placed = jnp.zeros((BLOCKS + 1, BLOCK, D), loaded.dtype).at[target].set(all_blocks)
    packed = placed[:BLOCKS].reshape(TOKENS, D)
    gate_proj = jnp.dot(packed, gate_weight, preferred_element_type=jnp.float32)
    up_proj = jnp.dot(packed, up_weight, preferred_element_type=jnp.float32)
    hidden = (jax.nn.silu(gate_proj) * up_proj).astype(jnp.bfloat16)
    summed = jnp.zeros((TOKENS, D), jnp.float32)
    for hid_group in range(FF // HID_DEV):
        first_unit = hid_group * HID_DEV
        partial_value = jnp.dot(hidden[:, first_unit:first_unit + HID_DEV], down_weight[first_unit:first_unit + HID_DEV], preferred_element_type=jnp.float32)
        summed = summed + lax.optimization_barrier(partial_value.astype(jnp.bfloat16)).astype(jnp.float32)
    return summed.astype(jnp.bfloat16)
```

```python
import functools

import jax
import jax.numpy as jnp
from jax import lax
from jax.experimental import pallas as pl
from jax.experimental.pallas import tpu as pltpu
from jax.sharding import PartitionSpec as P

BLOCK = 128
F32 = jnp.float32
BF16 = jnp.bfloat16
MIB = 1024 * 1024


def ring_order(n):
    if n == 8:
        return list(range(0, n, 2)) + list(range(n - 1, 0, -2))
    return list(range(n))


def shift(order, step):
    n = len(order)
    return [(order[i], order[(i + step) % n]) for i in range(n)]


def pack_kernel(mine_c, other_c, order, seq_at, mine, other, out, sems):
    loaders = mine_c.shape[0]
    blocks = order.shape[0]
    slots = mine.shape[0] // BLOCK // loaders
    own = out.shape[0] // BLOCK
    me = seq_at[0]

    first = [jnp.where(me == 0, mine_c[i], other_c[i]) for i in range(loaders)]
    second = [jnp.where(me == 0, other_c[i], mine_c[i]) for i in range(loaders)]
    counts = first + second
    copies = []
    for i in range(own):
        place = me * own + i
        source = jnp.int32(0)
        for b in range(blocks):
            source = jnp.where(order[b] == place, b, source)
        offset = jnp.int32(0)
        row = jnp.int32(0)
        for s in range(2 * loaders):
            inside = (source >= offset) & (source < offset + counts[s])
            row = jnp.where(inside, s * slots + source - offset, row)
            offset = offset + counts[s]
        holder = jnp.where(row >= loaders * slots, 1, 0)
        row = row - holder * (loaders * slots)
        start = pl.multiple_of(row * BLOCK, BLOCK)

        @pl.when(holder == me)
        def _(start=start, i=i):
            pltpu.make_async_copy(
                mine.at[pl.ds(start, BLOCK)], out.at[pl.ds(i * BLOCK, BLOCK)], sems.at[i]
            ).start()

        @pl.when(holder != me)
        def _(start=start, i=i):
            pltpu.make_async_copy(
                other.at[pl.ds(start, BLOCK)], out.at[pl.ds(i * BLOCK, BLOCK)], sems.at[i]
            ).start()

    for i in range(own):
        pltpu.make_async_copy(
            mine.at[pl.ds(0, BLOCK)], out.at[pl.ds(i * BLOCK, BLOCK)], sems.at[i]
        ).wait()


def pack(loaded, block_counts, seq_order):
    swap = [(0, 1), (1, 0)]
    other = lax.ppermute(loaded, "seq", swap)
    other_counts = lax.ppermute(block_counts, "seq", swap)
    own = seq_order.shape[0] // 2
    width = loaded.shape[1]
    seq_at = lax.axis_index("seq").astype(jnp.int32).reshape(1)
    any_spec = pl.BlockSpec(memory_space=pl.ANY)
    return pl.pallas_call(
        pack_kernel,
        out_shape=jax.ShapeDtypeStruct((own * BLOCK, width), loaded.dtype),
        grid_spec=pltpu.PrefetchScalarGridSpec(
            num_scalar_prefetch=4,
            grid=(1,),
            in_specs=[any_spec, any_spec],
            out_specs=any_spec,
            scratch_shapes=[pltpu.SemaphoreType.DMA((own,))],
        ),
    )(block_counts, other_counts, seq_order, seq_at, loaded, other)


def stage_kernel(pieces, has_acc, last, *refs):
    refs = list(refs[1:])
    xs = [(refs.pop(0), refs.pop(0)) for _ in range(pieces)]
    gws = [refs.pop(0) for _ in range(pieces)]
    uws = [refs.pop(0) for _ in range(pieces)]
    acc = [refs.pop(0), refs.pop(0)] if has_acc else None
    half = xs[0][0].shape[0]
    for c in range(2):
        rows = pl.ds(c * half, half)
        sums = []
        for k, ws in enumerate((gws, uws)):
            total = acc[k][rows, :] if has_acc else None
            for p in range(pieces):
                term = jnp.dot(xs[p][c][...], ws[p][...], preferred_element_type=F32)
                total = term if total is None else total + term
            sums.append(total)
        if last:
            gate, up = sums
            refs[0][rows, :] = (gate / (1.0 + jnp.exp(-gate)) * up).astype(BF16)
        else:
            refs[0][rows, :] = sums[0]
            refs[1][rows, :] = sums[1]


def stage(xs, owners, gate_weight, up_weight, acc, last, tile):
    pieces = len(xs)
    half, width = xs[0][0].shape
    hid = gate_weight.shape[1]
    x_spec = pl.BlockSpec((half, width), lambda i, own: (0, 0))
    w_specs = [
        pl.BlockSpec((width, tile), functools.partial(lambda p, i, own: (own[p], i), p))
        for p in range(pieces)
    ]
    full = pl.BlockSpec((2 * half, tile), lambda i, own: (0, i))
    operands = [x for pair in xs for x in pair] + [gate_weight] * pieces + [up_weight] * pieces
    in_specs = [x_spec] * (2 * pieces) + w_specs * 2
    aliases = {}
    if acc is not None:
        if not last:
            aliases = {1 + len(operands): 0, 2 + len(operands): 1}
        operands += list(acc)
        in_specs += [full, full]
    if last:
        out_shape = jax.ShapeDtypeStruct((2 * half, hid), BF16)
        out_specs = full
    else:
        out_shape = [jax.ShapeDtypeStruct((2 * half, hid), F32)] * 2
        out_specs = [full, full]
    return pl.pallas_call(
        functools.partial(stage_kernel, pieces, acc is not None, last),
        out_shape=out_shape,
        grid_spec=pltpu.PrefetchScalarGridSpec(
            num_scalar_prefetch=1,
            grid=(hid // tile,),
            in_specs=in_specs,
            out_specs=out_specs,
        ),
        input_output_aliases=aliases,
        compiler_params=pltpu.CompilerParams(vmem_limit_bytes=48 * MIB),
        cost_estimate=pl.CostEstimate(
            flops=2 * 2 * half * width * pieces * hid * 2,
            bytes_accessed=2 * width * pieces * hid * 2 + 2 * 2 * 2 * half * hid * 4,
            transcendentals=0,
        ),
    )(owners, *operands)


def body(loaded, block_counts, seq_order, gate_weight, up_weight, down_weight):
    n = lax.axis_size("tp")
    order = ring_order(n)
    table = jnp.array(order, jnp.int32)
    where = jnp.array([order.index(i) for i in range(n)], jnp.int32)
    at = where[lax.axis_index("tp")]
    fwd, bwd = shift(order, 1), shift(order, -1)
    far = n // 2

    def owner(step):
        return table[lax.rem(at + step + n, n)]

    packed = pack(loaded, block_counts, seq_order)
    half = packed.shape[0] // 2
    width = packed.shape[1]

    a_f = a_b = packed[:half]
    b_f = b_b = packed[half:]
    fresh = [((a_f, b_f), owner(0))]
    acc = None
    for step in range(1, far):
        a_f = lax.ppermute(a_f, "tp", fwd)
        a_b = lax.ppermute(a_b, "tp", bwd)
        b_f = lax.ppermute(b_f, "tp", fwd)
        b_b = lax.ppermute(b_b, "tp", bwd)
        fresh += [((a_f, b_f), owner(-step)), ((a_b, b_b), owner(step))]
        acc = stage(
            [x for x, _ in fresh],
            jnp.stack([o for _, o in fresh]),
            gate_weight, up_weight, acc, False, 256,
        )
        fresh = []
    a_f = lax.ppermute(a_f, "tp", fwd)
    b_b = lax.ppermute(b_b, "tp", bwd)
    hidden = stage([(a_f, b_b)], owner(far).reshape(1), gate_weight, up_weight, acc, True, 256)

    def term(rows, step):
        cols = lax.dynamic_slice_in_dim(down_weight, owner(step) * width, width, axis=1)
        return jnp.dot(rows, cols, preferred_element_type=F32)

    h_a, h_b = hidden[:half], hidden[half:]
    a_f = term(h_a, far).astype(BF16)
    b_b = term(h_b, far).astype(BF16)
    a_b = b_f = None
    for step in range(far - 1, 0, -1):
        a_f = lax.ppermute(a_f, "tp", fwd)
        b_b = lax.ppermute(b_b, "tp", bwd)
        if a_b is not None:
            a_b = lax.ppermute(a_b, "tp", bwd)
            b_f = lax.ppermute(b_f, "tp", fwd)
        a_f = (term(h_a, step) + a_f.astype(F32)).astype(BF16)
        b_b = (term(h_b, -step) + b_b.astype(F32)).astype(BF16)
        t_ab, t_bf = term(h_a, -step), term(h_b, step)
        a_b = (t_ab if a_b is None else t_ab + a_b.astype(F32)).astype(BF16)
        b_f = (t_bf if b_f is None else t_bf + b_f.astype(F32)).astype(BF16)
    a_f = lax.ppermute(a_f, "tp", fwd)
    b_b = lax.ppermute(b_b, "tp", bwd)
    a_b = lax.ppermute(a_b, "tp", bwd)
    b_f = lax.ppermute(b_f, "tp", fwd)
    out_a = term(h_a, 0) + a_f.astype(F32) + a_b.astype(F32)
    out_b = term(h_b, 0) + b_f.astype(F32) + b_b.astype(F32)
    return jnp.concatenate([out_a.astype(BF16), out_b.astype(BF16)], axis=0)


def solution(mesh):
    return jax.shard_map(
        body,
        mesh=mesh,
        in_specs=(
            P(("groups", "seq"), "tp"),
            P(("groups", "seq")),
            P("groups"),
            P(None, "tp"),
            P(None, "tp"),
            P("tp", None),
        ),
        out_specs=P(("groups", "seq"), "tp"),
        check_vma=False,
    )
```

```python
import functools

import jax
import jax.numpy as jnp
from jax import lax
from jax.experimental import pallas as pl
from jax.experimental.pallas import tpu as pltpu
from jax.sharding import PartitionSpec as P

BLOCK = 128
F32 = jnp.float32
BF16 = jnp.bfloat16
MIB = 1024 * 1024
VMEM = 32 * MIB


def ring_order(n):
    if n == 8:
        return list(range(0, n, 2)) + list(range(n - 1, 0, -2))
    return list(range(n))


def owner_at(step, n):
    here = lax.axis_index("tp")
    if n != 8:
        return (here + (step + n)) & (n - 1) if n & (n - 1) == 0 else lax.rem(here + (step + n), n)
    place = jnp.where((here & 1) == 0, here >> 1, n - 1 - (here >> 1))
    there = (place + (step + n)) & (n - 1)
    return jnp.where(there < n // 2, there * 2, 2 * n - 1 - 2 * there)


def shift(order, step):
    n = len(order)
    return [(order[i], order[(i + step) % n]) for i in range(n)]


def pack_kernel(mine_c, other_c, order, mine, other, first_half, second_half, sems):
    loaders = mine_c.shape[0]
    blocks = order.shape[0]
    slots = mine.shape[0] // BLOCK // loaders
    half = first_half.shape[0] // BLOCK
    own = 2 * half
    me = lax.axis_index("seq")

    first = [jnp.where(me == 0, mine_c[i], other_c[i]) for i in range(loaders)]
    second = [jnp.where(me == 0, other_c[i], mine_c[i]) for i in range(loaders)]
    counts = first + second
    copies = []
    for i in range(own):
        place = me * own + i
        source = jnp.int32(0)
        for b in range(blocks):
            source = jnp.where(order[b] == place, b, source)
        offset = jnp.int32(0)
        row = jnp.int32(0)
        for s in range(2 * loaders):
            inside = (source >= offset) & (source < offset + counts[s])
            row = jnp.where(inside, s * slots + source - offset, row)
            offset = offset + counts[s]
        holder = jnp.where(row >= loaders * slots, 1, 0)
        row = row - holder * (loaders * slots)
        start = pl.multiple_of(row * BLOCK, BLOCK)
        out = first_half if i < half else second_half
        at = pl.ds(i % half * BLOCK, BLOCK)

        @pl.when(holder == me)
        def _(start=start, i=i, out=out, at=at):
            pltpu.make_async_copy(
                mine.at[pl.ds(start, BLOCK)], out.at[at], sems.at[i]
            ).start()

        @pl.when(holder != me)
        def _(start=start, i=i, out=out, at=at):
            pltpu.make_async_copy(
                other.at[pl.ds(start, BLOCK)], out.at[at], sems.at[i]
            ).start()

    for i in range(own):
        out = first_half if i < half else second_half
        pltpu.make_async_copy(
            mine.at[pl.ds(0, BLOCK)], out.at[pl.ds(i % half * BLOCK, BLOCK)], sems.at[i]
        ).wait()


def pack(loaded, block_counts, seq_order):
    swap = [(0, 1), (1, 0)]
    other = lax.ppermute(loaded, "seq", swap)
    other_counts = lax.ppermute(block_counts, "seq", swap)
    own = seq_order.shape[0] // 2
    width = loaded.shape[1]
    rows = own // 2 * BLOCK
    any_spec = pl.BlockSpec(memory_space=pl.ANY)
    whole = pl.BlockSpec((rows, width), lambda i, *_: (0, 0))
    return pl.pallas_call(
        pack_kernel,
        out_shape=[jax.ShapeDtypeStruct((rows, width), loaded.dtype)] * 2,
        grid_spec=pltpu.PrefetchScalarGridSpec(
            num_scalar_prefetch=3,
            grid=(1,),
            in_specs=[any_spec, any_spec],
            out_specs=[whole, whole],
            scratch_shapes=[pltpu.SemaphoreType.DMA((own,))],
        ),
        compiler_params=pltpu.CompilerParams(vmem_limit_bytes=8 * MIB),
    )(block_counts, other_counts, seq_order, loaded, other)


def stage_kernel(pieces, has_acc, last, *refs):
    refs = list(refs)
    xs = [(refs.pop(0), refs.pop(0)) for _ in range(pieces)]
    gws = [refs.pop(0) for _ in range(pieces)]
    uws = [refs.pop(0) for _ in range(pieces)]
    acc = [refs.pop(0), refs.pop(0)] if has_acc else None
    half = xs[0][0].shape[0]
    for c in range(2):
        rows = pl.ds(c * half, half)
        sums = []
        for k, ws in enumerate((gws, uws)):
            total = acc[k][rows, :] if has_acc else None
            for p in range(pieces):
                term = jnp.dot(xs[p][c][...], ws[p][...], preferred_element_type=F32)
                total = term if total is None else total + term
            sums.append(total)
        if last:
            gate, up = sums
            refs[0][rows, :] = (gate / (1.0 + jnp.exp(-gate)) * up).astype(BF16)
        else:
            refs[0][rows, :] = sums[0]
            refs[1][rows, :] = sums[1]


def stage(xs, steps, gate_weight, up_weight, acc, last, tile):
    n = lax.axis_size("tp")
    pieces = len(xs)
    half, width = xs[0][0].shape
    hid = gate_weight.shape[1]
    x_spec = pl.BlockSpec((half, width), lambda i: (0, 0))
    w_specs = [
        pl.BlockSpec((width, tile), functools.partial(lambda s, i: (owner_at(s, n), i), s))
        for s in steps
    ]
    full = pl.BlockSpec((2 * half, tile), lambda i: (0, i))
    operands = [x for pair in xs for x in pair] + [gate_weight] * pieces + [up_weight] * pieces
    in_specs = [x_spec] * (2 * pieces) + w_specs * 2
    aliases = {}
    if acc is not None:
        if not last:
            aliases = {len(operands): 0, 1 + len(operands): 1}
        operands += list(acc)
        in_specs += [full, full]
    if last:
        out_shape = jax.ShapeDtypeStruct((2 * half, hid), BF16)
        out_specs = full
    else:
        out_shape = [jax.ShapeDtypeStruct((2 * half, hid), F32)] * 2
        out_specs = [full, full]
    return pl.pallas_call(
        functools.partial(stage_kernel, pieces, acc is not None, last),
        out_shape=out_shape,
        grid=(hid // tile,),
        in_specs=in_specs,
        out_specs=out_specs,
        input_output_aliases=aliases,
        compiler_params=pltpu.CompilerParams(vmem_limit_bytes=VMEM),
        cost_estimate=pl.CostEstimate(
            flops=2 * 2 * half * width * pieces * hid * 2,
            bytes_accessed=2 * width * pieces * hid * 2 + 2 * 2 * 2 * half * hid * 4,
            transcendentals=0,
        ),
    )(*operands)


def body(loaded, block_counts, seq_order, gate_weight, up_weight, down_weight):
    n = lax.axis_size("tp")
    order = ring_order(n)
    fwd, bwd = shift(order, 1), shift(order, -1)
    far = n // 2

    own_a, own_b = pack(loaded, block_counts, seq_order)
    half, width = own_a.shape

    a_f = a_b = own_a
    b_f = b_b = own_b
    fresh = [((a_f, b_f), 0)]
    acc = None
    for step in range(1, far):
        a_f = lax.ppermute(a_f, "tp", fwd)
        a_b = lax.ppermute(a_b, "tp", bwd)
        b_f = lax.ppermute(b_f, "tp", fwd)
        b_b = lax.ppermute(b_b, "tp", bwd)
        fresh += [((a_f, b_f), -step), ((a_b, b_b), step)]
        acc = stage(
            [x for x, _ in fresh],
            [o for _, o in fresh],
            gate_weight, up_weight, acc, False, 896,
        )
        fresh = []
    a_f = lax.ppermute(a_f, "tp", fwd)
    b_b = lax.ppermute(b_b, "tp", bwd)
    hidden = stage([(a_f, b_b)], [far], gate_weight, up_weight, acc, True, 896)

    def term(rows, step):
        cols = lax.dynamic_slice_in_dim(down_weight, owner_at(step, n) * width, width, axis=1)
        return jnp.dot(rows, cols, preferred_element_type=F32)

    h_a, h_b = hidden[:half], hidden[half:]
    a_f = term(h_a, far).astype(BF16)
    b_b = term(h_b, far).astype(BF16)
    a_b = b_f = None
    for step in range(far - 1, 0, -1):
        a_f = lax.ppermute(a_f, "tp", fwd)
        b_b = lax.ppermute(b_b, "tp", bwd)
        if a_b is not None:
            a_b = lax.ppermute(a_b, "tp", bwd)
            b_f = lax.ppermute(b_f, "tp", fwd)
        a_f = (term(h_a, step) + a_f.astype(F32)).astype(BF16)
        b_b = (term(h_b, -step) + b_b.astype(F32)).astype(BF16)
        t_ab, t_bf = term(h_a, -step), term(h_b, step)
        a_b = (t_ab if a_b is None else t_ab + a_b.astype(F32)).astype(BF16)
        b_f = (t_bf if b_f is None else t_bf + b_f.astype(F32)).astype(BF16)
    a_f = lax.ppermute(a_f, "tp", fwd)
    b_b = lax.ppermute(b_b, "tp", bwd)
    a_b = lax.ppermute(a_b, "tp", bwd)
    b_f = lax.ppermute(b_f, "tp", fwd)
    out_a = term(h_a, 0) + a_f.astype(F32) + a_b.astype(F32)
    out_b = term(h_b, 0) + b_f.astype(F32) + b_b.astype(F32)
    return jnp.concatenate([out_a.astype(BF16), out_b.astype(BF16)], axis=0)


def solution(mesh):
    return jax.shard_map(
        body,
        mesh=mesh,
        in_specs=(
            P(("groups", "seq"), "tp"),
            P(("groups", "seq")),
            P("groups"),
            P(None, "tp"),
            P(None, "tp"),
            P("tp", None),
        ),
        out_specs=P(("groups", "seq"), "tp"),
        check_vma=False,
    )
```

```python
import functools

import jax
import jax.numpy as jnp
from jax import lax
from jax.experimental import pallas as pl
from jax.experimental.pallas import tpu as pltpu
from jax.sharding import PartitionSpec as P

BLOCK = 128
F32 = jnp.float32
BF16 = jnp.bfloat16
MIB = 1024 * 1024
IN_VMEM = pl.BlockSpec(memory_space=pltpu.VMEM)


def ring_order(n):
    if n == 8:
        return list(range(0, n, 2)) + list(range(n - 1, 0, -2))
    return list(range(n))


def owner_at(step, n):
    here = lax.axis_index("tp")
    if n != 8:
        return (here + (step + n)) & (n - 1) if n & (n - 1) == 0 else lax.rem(here + (step + n), n)
    place = jnp.where((here & 1) == 0, here >> 1, n - 1 - (here >> 1))
    there = (place + (step + n)) & (n - 1)
    return jnp.where(there < n // 2, there * 2, 2 * n - 1 - 2 * there)


def shift(order, step):
    n = len(order)
    return [(order[i], order[(i + step) % n]) for i in range(n)]


def in_hbm(x):
    return pltpu.with_memory_space_constraint(x, pltpu.HBM)


def pack_kernel(mine_c, other_c, order, mine, other, _, first_half, second_half, sems):
    loaders = mine_c.shape[0]
    blocks = order.shape[0]
    slots = mine.shape[0] // BLOCK // loaders
    half = first_half.shape[0] // BLOCK
    own = 2 * half
    me = lax.axis_index("seq")

    first = [jnp.where(me == 0, mine_c[i], other_c[i]) for i in range(loaders)]
    second = [jnp.where(me == 0, other_c[i], mine_c[i]) for i in range(loaders)]
    counts = first + second
    copies = []
    for i in range(own):
        place = me * own + i
        source = jnp.int32(0)
        for b in range(blocks):
            source = jnp.where(order[b] == place, b, source)
        offset = jnp.int32(0)
        row = jnp.int32(0)
        for s in range(2 * loaders):
            inside = (source >= offset) & (source < offset + counts[s])
            row = jnp.where(inside, s * slots + source - offset, row)
            offset = offset + counts[s]
        holder = jnp.where(row >= loaders * slots, 1, 0)
        row = row - holder * (loaders * slots)
        start = pl.multiple_of(row * BLOCK, BLOCK)
        out = first_half if i < half else second_half
        at = pl.ds(i % half * BLOCK, BLOCK)

        @pl.when(holder == me)
        def _(start=start, i=i, out=out, at=at):
            pltpu.make_async_copy(
                mine.at[pl.ds(start, BLOCK)], out.at[at], sems.at[i]
            ).start()

        @pl.when(holder != me)
        def _(start=start, i=i, out=out, at=at):
            pltpu.make_async_copy(
                other.at[pl.ds(start, BLOCK)], out.at[at], sems.at[i]
            ).start()

    for i in range(own):
        out = first_half if i < half else second_half
        pltpu.make_async_copy(
            mine.at[pl.ds(0, BLOCK)], out.at[pl.ds(i % half * BLOCK, BLOCK)], sems.at[i]
        ).wait()


def pack(loaded, block_counts, seq_order, after):
    swap = [(0, 1), (1, 0)]
    other = lax.ppermute(loaded, "seq", swap)
    other_counts = lax.ppermute(block_counts, "seq", swap)
    own = seq_order.shape[0] // 2
    width = loaded.shape[1]
    rows = own // 2 * BLOCK
    any_spec = pl.BlockSpec(memory_space=pl.ANY)
    whole = pl.BlockSpec((rows, width), lambda i, *_: (0, 0))
    return pl.pallas_call(
        pack_kernel,
        out_shape=[jax.ShapeDtypeStruct((rows, width), loaded.dtype)] * 2,
        grid_spec=pltpu.PrefetchScalarGridSpec(
            num_scalar_prefetch=3,
            grid=(1,),
            in_specs=[any_spec, any_spec, IN_VMEM],
            out_specs=[whole, whole],
            scratch_shapes=[pltpu.SemaphoreType.DMA((own,))],
        ),
        compiler_params=pltpu.CompilerParams(vmem_limit_bytes=8 * MIB),
    )(in_hbm(block_counts), other_counts, in_hbm(seq_order), in_hbm(loaded), other, after)


GATE, UP, DOWN = range(3)


def bring_start(bring, n, sources, targets, sems):
    copies = []
    for i, (which, step) in enumerate(bring):
        rows, cols = targets[i].shape
        source = sources[which]
        if which == DOWN:
            piece = source.at[:, pl.ds(pl.multiple_of(owner_at(step, n) * cols, cols), cols)]
        else:
            piece = source.at[pl.ds(pl.multiple_of(owner_at(step, n) * rows, rows), rows)]
        copies.append(pltpu.make_async_copy(piece, targets[i], sems.at[i]))
        copies[-1].start()
    return copies


def brought(bring, sources, n):
    shapes = []
    for which, _ in bring:
        rows, cols = sources[which].shape
        shape = (rows, cols // n) if which == DOWN else (rows // n, cols)
        shapes.append(pltpu.VMEM(shape, sources[which].dtype))
    return shapes


def fetch_kernel(bring, n, has_after, *refs):
    first = 3 + has_after
    for copy in bring_start(bring, n, refs[:3], refs[first:-1], refs[-1]):
        copy.wait()


def fetch(sources, bring, after=None):
    n = lax.axis_size("tp")
    outs = brought(bring, sources, n)
    any_spec = pl.BlockSpec(memory_space=pl.ANY)
    more = [] if after is None else [after]
    out = pl.pallas_call(
        functools.partial(fetch_kernel, bring, n, len(more)),
        out_shape=outs,
        in_specs=[any_spec] * 3 + [IN_VMEM] * len(more),
        out_specs=[IN_VMEM] * len(outs),
        scratch_shapes=[pltpu.SemaphoreType.DMA((len(bring),))],
        compiler_params=pltpu.CompilerParams(vmem_limit_bytes=MIB),
        cost_estimate=pl.CostEstimate(
            flops=0, bytes_accessed=len(bring) * 4 * MIB, transcendentals=0
        ),
    )(*sources, *more)
    return dict(zip(bring, out))


def stage_kernel(pieces, has_acc, last, bring, n, *refs):
    refs = list(refs)
    if bring:
        sems = refs.pop()
        sources = [refs.pop(0) for _ in range(3)]
        targets = refs[-len(bring) :]
        bring_start(bring, n, sources, targets, sems)
    xs = [refs.pop(0) for _ in range(pieces)]
    weights = [[refs.pop(0) for _ in range(pieces)] for _ in range(2)]
    acc = [refs.pop(0), refs.pop(0)] if has_acc else None

    def columns(start, tile):
        cols = pl.ds(start, tile)
        sums = []
        for k in range(2):
            total = acc[k][:, cols] if has_acc else None
            for x, weight in zip(xs, weights[k]):
                term = jnp.dot(x[...], weight[:, cols], preferred_element_type=F32)
                total = term if total is None else total + term
            sums.append(total)
        if last:
            gate, up = sums
            refs[0][:, cols] = (gate / (1.0 + jnp.exp(-gate)) * up).astype(BF16)
        else:
            refs[0][:, cols] = sums[0]
            refs[1][:, cols] = sums[1]

    lanes = weights[0][0].shape[1] // 128
    if bring:
        count = next(c for c in range(2, lanes + 1) if lanes % c == 0)
        tile = lanes // count * 128
        pl.loop(0, count)(lambda i: columns(pl.multiple_of(i * tile, tile), tile))
    else:
        tile = 256 if lanes % 2 == 0 else 128
        for i in range(lanes * 128 // tile):
            columns(i * tile, tile)
    if bring:
        for i, target in enumerate(targets):
            pltpu.make_async_copy(target, target, sems.at[i]).wait()


def stage(held, sources, xs, steps, acc=(), last=False, bring=()):
    n = lax.axis_size("tp")
    rows, width = xs[0].shape
    hid = sources[GATE].shape[1]
    operands = [*xs, *[held[which, step] for which in (GATE, UP) for step in steps], *acc]
    if last:
        out_shape = [pltpu.VMEM((rows, hid), BF16)]
    else:
        out_shape = [pltpu.VMEM((rows, hid), F32)] * 2
    outs = len(out_shape)
    in_specs = [IN_VMEM] * len(operands)
    scratch = []
    if bring:
        operands = [*sources, *operands]
        in_specs = [pl.BlockSpec(memory_space=pl.ANY)] * 3 + in_specs
        out_shape += brought(bring, sources, n)
        scratch = [pltpu.SemaphoreType.DMA((len(bring),))]
    aliases = {len(operands) - 2: 0, len(operands) - 1: 1} if acc and not last else {}
    out = pl.pallas_call(
        functools.partial(stage_kernel, len(xs), bool(acc), last, bring, n),
        out_shape=out_shape,
        in_specs=in_specs,
        out_specs=[IN_VMEM] * len(out_shape),
        scratch_shapes=scratch,
        input_output_aliases=aliases,
        compiler_params=pltpu.CompilerParams(vmem_limit_bytes=4 * MIB),
        cost_estimate=pl.CostEstimate(
            flops=4 * rows * width * len(xs) * hid, bytes_accessed=0, transcendentals=0
        ),
    )(*operands)
    held.update(zip(bring, out[outs:]))
    return out[:outs]


def down_kernel(h, weight, *refs):
    total = jnp.dot(h[...], weight[...], preferred_element_type=F32)
    for other in refs[:-1]:
        total = total + other[...].astype(F32)
    refs[-1][...] = total.astype(refs[-1].dtype)


def down(h, weight, *arrived, dtype=BF16):
    operands = [h, weight, *arrived]
    return pl.pallas_call(
        down_kernel,
        out_shape=jax.ShapeDtypeStruct((h.shape[0], weight.shape[1]), dtype),
        in_specs=[IN_VMEM] * len(operands),
        out_specs=IN_VMEM,
        compiler_params=pltpu.CompilerParams(vmem_limit_bytes=4 * MIB),
        cost_estimate=pl.CostEstimate(
            flops=2 * h.size * weight.shape[1], bytes_accessed=0, transcendentals=0
        ),
    )(*operands)


def finish_kernel(own_a, own_b, a_f, a_b, b_f, b_b, out):
    half = own_a.shape[0]
    for i, (own, f, b) in enumerate(((own_a, a_f, a_b), (own_b, b_f, b_b))):
        total = own[...] + f[...].astype(F32) + b[...].astype(F32)
        out[i * half : (i + 1) * half, :] = total.astype(BF16)


def finish(own_a, own_b, arrived_a, arrived_b):
    rows, width = own_a.shape
    return pl.pallas_call(
        finish_kernel,
        out_shape=jax.ShapeDtypeStruct((2 * rows, width), BF16),
        in_specs=[IN_VMEM] * 6,
        out_specs=IN_VMEM,
        compiler_params=pltpu.CompilerParams(vmem_limit_bytes=8 * MIB),
    )(own_a, own_b, *arrived_a, *arrived_b)


def both(*steps):
    return tuple((which, step) for step in steps for which in (GATE, UP))


def body(loaded, block_counts, seq_order, gate_weight, up_weight, down_weight):
    n = lax.axis_size("tp")
    order = ring_order(n)
    fwd, bwd = shift(order, 1), shift(order, -1)
    far = n // 2
    sources = [in_hbm(w) for w in (gate_weight, up_weight, down_weight)]

    later = [slot for step in range(3, far) for slot in both(step, -step)] + list(both(far))
    later += [(DOWN, far)]
    for step in range(far - 1, 0, -1):
        later += [(DOWN, step), (DOWN, -step)]
    later += [(DOWN, 0)]
    stages = 2 * (far - 1)
    shares = [
        tuple(later[i * len(later) // stages : (i + 1) * len(later) // stages])
        for i in range(stages)
    ]

    held = fetch(sources, both(0))
    own_a, own_b = pack(loaded, block_counts, seq_order, held[GATE, 0])
    run = functools.partial(stage, held, sources)

    a_f = a_b = own_a
    b_f = b_b = own_b
    acc_a = run([own_a], [0], bring=both(1))
    acc_b = run([own_b], [0], bring=both(-1))
    held |= fetch(sources, both(2, -2), acc_b[0])
    for step in range(1, far):
        a_f = lax.ppermute(a_f, "tp", fwd)
        a_b = lax.ppermute(a_b, "tp", bwd)
        b_f = lax.ppermute(b_f, "tp", fwd)
        b_b = lax.ppermute(b_b, "tp", bwd)
        acc_a = run([a_f, a_b], [-step, step], acc_a, bring=shares[2 * step - 2])
        acc_b = run([b_f, b_b], [-step, step], acc_b, bring=shares[2 * step - 1])
    a_f = lax.ppermute(a_f, "tp", fwd)
    b_b = lax.ppermute(b_b, "tp", bwd)
    (h_a,) = run([a_f], [far], acc_a, last=True)
    (h_b,) = run([b_b], [far], acc_b, last=True)

    def term_a(step, *arrived):
        return down(h_a, held[DOWN, step], *arrived)

    def term_b(step, *arrived):
        return down(h_b, held[DOWN, step], *arrived)

    a_f, b_b = term_a(far), term_b(far)
    a_b, b_f = term_a(1 - far), term_b(far - 1)
    for step in range(far - 1, 0, -1):
        a_f = term_a(step, lax.ppermute(a_f, "tp", fwd))
        b_b = term_b(-step, lax.ppermute(b_b, "tp", bwd))
        if step > 1:
            a_b = term_a(1 - step, lax.ppermute(a_b, "tp", bwd))
            b_f = term_b(step - 1, lax.ppermute(b_f, "tp", fwd))
    last = held[DOWN, 0]
    own = down(h_a, last, dtype=F32), down(h_b, last, dtype=F32)
    return finish(
        *own,
        (lax.ppermute(a_f, "tp", fwd), lax.ppermute(a_b, "tp", bwd)),
        (lax.ppermute(b_f, "tp", fwd), lax.ppermute(b_b, "tp", bwd)),
    )


def solution(mesh):
    return jax.shard_map(
        body,
        mesh=mesh,
        in_specs=(
            P(("groups", "seq"), "tp"),
            P(("groups", "seq")),
            P("groups"),
            P(None, "tp"),
            P(None, "tp"),
            P("tp", None),
        ),
        out_specs=P(("groups", "seq"), "tp"),
        check_vma=False,
    )
```

```python
import functools

import jax
import jax.numpy as jnp
from jax import lax
from jax.experimental import pallas as pl
from jax.experimental.pallas import tpu as pltpu
from jax.sharding import PartitionSpec as P

BLOCK = 128
F32 = jnp.float32
BF16 = jnp.bfloat16
MIB = 1024 * 1024
IN_VMEM = pl.BlockSpec(memory_space=pltpu.VMEM)


def ring_order(n):
    if n == 8:
        return list(range(0, n, 2)) + list(range(n - 1, 0, -2))
    return list(range(n))


def owner_at(step, n):
    here = lax.axis_index("tp")
    if n != 8:
        return (here + (step + n)) & (n - 1) if n & (n - 1) == 0 else lax.rem(here + (step + n), n)
    place = jnp.where((here & 1) == 0, here >> 1, n - 1 - (here >> 1))
    there = (place + (step + n)) & (n - 1)
    return jnp.where(there < n // 2, there * 2, 2 * n - 1 - 2 * there)


def shift(order, step):
    n = len(order)
    return [(order[i], order[(i + step) % n]) for i in range(n)]


def in_hbm(x):
    return pltpu.with_memory_space_constraint(x, pltpu.HBM)


def pack_kernel(mine_c, other_c, order, mine, other, _, first_half, second_half, sems):
    loaders = mine_c.shape[0]
    blocks = order.shape[0]
    slots = mine.shape[0] // BLOCK // loaders
    half = first_half.shape[0] // BLOCK
    own = 2 * half
    me = lax.axis_index("seq")

    first = [jnp.where(me == 0, mine_c[i], other_c[i]) for i in range(loaders)]
    second = [jnp.where(me == 0, other_c[i], mine_c[i]) for i in range(loaders)]
    counts = first + second
    copies = []
    for i in range(own):
        place = me * own + i
        source = jnp.int32(0)
        for b in range(blocks):
            source = jnp.where(order[b] == place, b, source)
        offset = jnp.int32(0)
        row = jnp.int32(0)
        for s in range(2 * loaders):
            inside = (source >= offset) & (source < offset + counts[s])
            row = jnp.where(inside, s * slots + source - offset, row)
            offset = offset + counts[s]
        holder = jnp.where(row >= loaders * slots, 1, 0)
        row = row - holder * (loaders * slots)
        start = pl.multiple_of(row * BLOCK, BLOCK)
        out = first_half if i < half else second_half
        at = pl.ds(i % half * BLOCK, BLOCK)

        @pl.when(holder == me)
        def _(start=start, i=i, out=out, at=at):
            pltpu.make_async_copy(
                mine.at[pl.ds(start, BLOCK)], out.at[at], sems.at[i]
            ).start()

        @pl.when(holder != me)
        def _(start=start, i=i, out=out, at=at):
            pltpu.make_async_copy(
                other.at[pl.ds(start, BLOCK)], out.at[at], sems.at[i]
            ).start()

    for i in range(own):
        out = first_half if i < half else second_half
        pltpu.make_async_copy(
            mine.at[pl.ds(0, BLOCK)], out.at[pl.ds(i % half * BLOCK, BLOCK)], sems.at[i]
        ).wait()


def pack(loaded, block_counts, seq_order, after):
    swap = [(0, 1), (1, 0)]
    other = lax.ppermute(loaded, "seq", swap)
    other_counts = lax.ppermute(block_counts, "seq", swap)
    own = seq_order.shape[0] // 2
    width = loaded.shape[1]
    rows = own // 2 * BLOCK
    any_spec = pl.BlockSpec(memory_space=pl.ANY)
    whole = pl.BlockSpec((rows, width), lambda i, *_: (0, 0))
    return pl.pallas_call(
        pack_kernel,
        out_shape=[jax.ShapeDtypeStruct((rows, width), loaded.dtype)] * 2,
        grid_spec=pltpu.PrefetchScalarGridSpec(
            num_scalar_prefetch=3,
            grid=(1,),
            in_specs=[any_spec, any_spec, IN_VMEM],
            out_specs=[whole, whole],
            scratch_shapes=[pltpu.SemaphoreType.DMA((own,))],
        ),
        compiler_params=pltpu.CompilerParams(vmem_limit_bytes=8 * MIB),
    )(in_hbm(block_counts), other_counts, in_hbm(seq_order), in_hbm(loaded), other, after)


GATE, UP, DOWN = range(3)


def bring_start(bring, n, sources, targets, sems):
    copies = []
    for i, (which, step) in enumerate(bring):
        rows, cols = targets[i].shape
        source = sources[which]
        if which == DOWN:
            piece = source.at[:, pl.ds(pl.multiple_of(owner_at(step, n) * cols, cols), cols)]
        else:
            piece = source.at[pl.ds(pl.multiple_of(owner_at(step, n) * rows, rows), rows)]
        copies.append(pltpu.make_async_copy(piece, targets[i], sems.at[i]))
        copies[-1].start()
    return copies


def brought(bring, sources, n):
    shapes = []
    for which, _ in bring:
        rows, cols = sources[which].shape
        shape = (rows, cols // n) if which == DOWN else (rows // n, cols)
        shapes.append(pltpu.VMEM(shape, sources[which].dtype))
    return shapes


def fetch_kernel(bring, n, has_after, *refs):
    first = 3 + has_after
    for copy in bring_start(bring, n, refs[:3], refs[first:-1], refs[-1]):
        copy.wait()


def fetch(sources, bring, after=None):
    n = lax.axis_size("tp")
    outs = brought(bring, sources, n)
    any_spec = pl.BlockSpec(memory_space=pl.ANY)
    more = [] if after is None else [after]
    out = pl.pallas_call(
        functools.partial(fetch_kernel, bring, n, len(more)),
        out_shape=outs,
        in_specs=[any_spec] * 3 + [IN_VMEM] * len(more),
        out_specs=[IN_VMEM] * len(outs),
        scratch_shapes=[pltpu.SemaphoreType.DMA((len(bring),))],
        compiler_params=pltpu.CompilerParams(vmem_limit_bytes=MIB),
        cost_estimate=pl.CostEstimate(
            flops=0, bytes_accessed=len(bring) * 4 * MIB, transcendentals=0
        ),
    )(*sources, *more)
    return dict(zip(bring, out))


def stage_kernel(pieces, has_acc, last, bring, n, *refs):
    refs = list(refs)
    if bring:
        sems = refs.pop()
        sources = [refs.pop(0) for _ in range(3)]
        targets = refs[-len(bring) :]
        bring_start(bring, n, sources, targets, sems)
    xs = [refs.pop(0) for _ in range(pieces)]
    weights = [[refs.pop(0) for _ in range(pieces)] for _ in range(2)]
    acc = [refs.pop(0), refs.pop(0)] if has_acc else None

    def columns(start, tile):
        cols = pl.ds(start, tile)
        sums = []
        for k in range(2):
            total = acc[k][:, cols] if has_acc else None
            for x, weight in zip(xs, weights[k]):
                term = jnp.dot(x[...], weight[:, cols], preferred_element_type=F32)
                total = term if total is None else total + term
            sums.append(total)
        if last:
            gate, up = sums
            refs[0][:, cols] = (gate / (1.0 + jnp.exp(-gate)) * up).astype(BF16)
        else:
            refs[0][:, cols] = sums[0]
            refs[1][:, cols] = sums[1]

    lanes = weights[0][0].shape[1] // 128
    if bring:
        count = next(c for c in range(2, lanes + 1) if lanes % c == 0)
        tile = lanes // count * 128
        pl.loop(0, count)(lambda i: columns(pl.multiple_of(i * tile, tile), tile))
    else:
        tile = 256 if lanes % 2 == 0 else 128
        for i in range(lanes * 128 // tile):
            columns(i * tile, tile)
    if bring:
        for i, target in enumerate(targets):
            pltpu.make_async_copy(target, target, sems.at[i]).wait()


def stage(held, sources, xs, steps, acc=(), last=False, bring=()):
    n = lax.axis_size("tp")
    rows, width = xs[0].shape
    hid = sources[GATE].shape[1]
    operands = [*xs, *[held[which, step] for which in (GATE, UP) for step in steps], *acc]
    if last:
        out_shape = [pltpu.VMEM((rows, hid), BF16)]
    else:
        out_shape = [pltpu.VMEM((rows, hid), F32)] * 2
    outs = len(out_shape)
    in_specs = [IN_VMEM] * len(operands)
    scratch = []
    if bring:
        operands = [*sources, *operands]
        in_specs = [pl.BlockSpec(memory_space=pl.ANY)] * 3 + in_specs
        out_shape += brought(bring, sources, n)
        scratch = [pltpu.SemaphoreType.DMA((len(bring),))]
    aliases = {len(operands) - 2: 0, len(operands) - 1: 1} if acc and not last else {}
    out = pl.pallas_call(
        functools.partial(stage_kernel, len(xs), bool(acc), last, bring, n),
        out_shape=out_shape,
        in_specs=in_specs,
        out_specs=[IN_VMEM] * len(out_shape),
        scratch_shapes=scratch,
        input_output_aliases=aliases,
        compiler_params=pltpu.CompilerParams(vmem_limit_bytes=4 * MIB),
        cost_estimate=pl.CostEstimate(
            flops=12 * rows * width * len(xs) * hid, bytes_accessed=0, transcendentals=0
        ),
    )(*operands)
    held.update(zip(bring, out[outs:]))
    return out[:outs]


def down_kernel(h, weight, *refs):
    total = jnp.dot(h[...], weight[...], preferred_element_type=F32)
    for other in refs[:-1]:
        total = total + other[...].astype(F32)
    refs[-1][...] = total.astype(refs[-1].dtype)


def down(h, weight, *arrived, dtype=BF16):
    operands = [h, weight, *arrived]
    return pl.pallas_call(
        down_kernel,
        out_shape=jax.ShapeDtypeStruct((h.shape[0], weight.shape[1]), dtype),
        in_specs=[IN_VMEM] * len(operands),
        out_specs=IN_VMEM,
        compiler_params=pltpu.CompilerParams(vmem_limit_bytes=4 * MIB),
        cost_estimate=pl.CostEstimate(
            flops=6 * h.size * weight.shape[1], bytes_accessed=0, transcendentals=0
        ),
    )(*operands)


def finish_kernel(own_a, own_b, a_f, a_b, b_f, b_b, out):
    half = own_a.shape[0]
    for i, (own, f, b) in enumerate(((own_a, a_f, a_b), (own_b, b_f, b_b))):
        total = own[...] + f[...].astype(F32) + b[...].astype(F32)
        out[i * half : (i + 1) * half, :] = total.astype(BF16)


def finish(own_a, own_b, arrived_a, arrived_b):
    rows, width = own_a.shape
    return pl.pallas_call(
        finish_kernel,
        out_shape=jax.ShapeDtypeStruct((2 * rows, width), BF16),
        in_specs=[IN_VMEM] * 6,
        out_specs=IN_VMEM,
        compiler_params=pltpu.CompilerParams(vmem_limit_bytes=8 * MIB),
    )(own_a, own_b, *arrived_a, *arrived_b)


def both(*steps):
    return tuple((which, step) for step in steps for which in (GATE, UP))


def body(loaded, block_counts, seq_order, gate_weight, up_weight, down_weight):
    n = lax.axis_size("tp")
    order = ring_order(n)
    fwd, bwd = shift(order, 1), shift(order, -1)
    far = n // 2
    sources = [in_hbm(w) for w in (gate_weight, up_weight, down_weight)]

    later = [slot for step in range(3, far) for slot in both(step, -step)] + list(both(far))
    later += [(DOWN, far)]
    for step in range(far - 1, 0, -1):
        later += [(DOWN, step), (DOWN, -step)]
    later += [(DOWN, 0)]
    stages = 2 * (far - 1)
    shares = [
        tuple(later[i * len(later) // stages : (i + 1) * len(later) // stages])
        for i in range(stages)
    ]

    held = fetch(sources, both(0))
    own_a, own_b = pack(loaded, block_counts, seq_order, held[GATE, 0])
    run = functools.partial(stage, held, sources)

    a_f = a_b = own_a
    b_f = b_b = own_b
    acc_a = run([own_a], [0], bring=both(1))
    acc_b = run([own_b], [0], bring=both(-1))
    held |= fetch(sources, both(2, -2), acc_b[0])
    for step in range(1, far):
        a_f = lax.ppermute(a_f, "tp", fwd)
        a_b = lax.ppermute(a_b, "tp", bwd)
        b_f = lax.ppermute(b_f, "tp", fwd)
        b_b = lax.ppermute(b_b, "tp", bwd)
        acc_a = run([a_f, a_b], [-step, step], acc_a, bring=shares[2 * step - 2])
        acc_b = run([b_f, b_b], [-step, step], acc_b, bring=shares[2 * step - 1])
    a_f = lax.ppermute(a_f, "tp", fwd)
    b_b = lax.ppermute(b_b, "tp", bwd)
    (h_a,) = run([a_f], [far], acc_a, last=True)
    (h_b,) = run([b_b], [far], acc_b, last=True)

    def term_a(step, *arrived):
        return down(h_a, held[DOWN, step], *arrived)

    def term_b(step, *arrived):
        return down(h_b, held[DOWN, step], *arrived)

    a_f, b_b = term_a(far), term_b(far)
    a_b, b_f = term_a(1 - far), term_b(far - 1)
    for step in range(far - 1, 0, -1):
        a_f = term_a(step, lax.ppermute(a_f, "tp", fwd))
        b_b = term_b(-step, lax.ppermute(b_b, "tp", bwd))
        if step > 1:
            a_b = term_a(1 - step, lax.ppermute(a_b, "tp", bwd))
            b_f = term_b(step - 1, lax.ppermute(b_f, "tp", fwd))
    last = held[DOWN, 0]
    own = down(h_a, last, dtype=F32), down(h_b, last, dtype=F32)
    return finish(
        *own,
        (lax.ppermute(a_f, "tp", fwd), lax.ppermute(a_b, "tp", bwd)),
        (lax.ppermute(b_f, "tp", fwd), lax.ppermute(b_b, "tp", bwd)),
    )


def solution(mesh):
    return jax.shard_map(
        body,
        mesh=mesh,
        in_specs=(
            P(("groups", "seq"), "tp"),
            P(("groups", "seq")),
            P("groups"),
            P(None, "tp"),
            P(None, "tp"),
            P("tp", None),
        ),
        out_specs=P(("groups", "seq"), "tp"),
        check_vma=False,
    )
```

```python
import functools

import jax
import jax.numpy as jnp
from jax import lax
from jax.experimental import pallas as pl
from jax.experimental.pallas import tpu as pltpu
from jax.sharding import PartitionSpec as P

BLOCK = 128
F32 = jnp.float32
BF16 = jnp.bfloat16
MIB = 1024 * 1024
IN_VMEM = pl.BlockSpec(memory_space=pltpu.VMEM)


def ring_order(n):
    if n == 8:
        return list(range(0, n, 2)) + list(range(n - 1, 0, -2))
    return list(range(n))


def owner_at(step, n):
    here = lax.axis_index("tp")
    if n != 8:
        return (here + (step + n)) & (n - 1) if n & (n - 1) == 0 else lax.rem(here + (step + n), n)
    place = jnp.where((here & 1) == 0, here >> 1, n - 1 - (here >> 1))
    there = (place + (step + n)) & (n - 1)
    return jnp.where(there < n // 2, there * 2, 2 * n - 1 - 2 * there)


def shift(order, step):
    n = len(order)
    return [(order[i], order[(i + step) % n]) for i in range(n)]


def in_hbm(x):
    return pltpu.with_memory_space_constraint(x, pltpu.HBM)


def pack_kernel(mine_c, other_c, order, mine, other, _, first_half, second_half, sems):
    loaders = mine_c.shape[0]
    blocks = order.shape[0]
    slots = mine.shape[0] // BLOCK // loaders
    half = first_half.shape[0] // BLOCK
    own = 2 * half
    me = lax.axis_index("seq")

    first = [jnp.where(me == 0, mine_c[i], other_c[i]) for i in range(loaders)]
    second = [jnp.where(me == 0, other_c[i], mine_c[i]) for i in range(loaders)]
    counts = first + second
    copies = []
    for i in range(own):
        place = me * own + i
        source = jnp.int32(0)
        for b in range(blocks):
            source = jnp.where(order[b] == place, b, source)
        offset = jnp.int32(0)
        row = jnp.int32(0)
        for s in range(2 * loaders):
            inside = (source >= offset) & (source < offset + counts[s])
            row = jnp.where(inside, s * slots + source - offset, row)
            offset = offset + counts[s]
        holder = jnp.where(row >= loaders * slots, 1, 0)
        row = row - holder * (loaders * slots)
        start = pl.multiple_of(row * BLOCK, BLOCK)
        out = first_half if i < half else second_half
        at = pl.ds(i % half * BLOCK, BLOCK)

        @pl.when(holder == me)
        def _(start=start, i=i, out=out, at=at):
            pltpu.make_async_copy(
                mine.at[pl.ds(start, BLOCK)], out.at[at], sems.at[i]
            ).start()

        @pl.when(holder != me)
        def _(start=start, i=i, out=out, at=at):
            pltpu.make_async_copy(
                other.at[pl.ds(start, BLOCK)], out.at[at], sems.at[i]
            ).start()

    for i in range(own):
        out = first_half if i < half else second_half
        pltpu.make_async_copy(
            mine.at[pl.ds(0, BLOCK)], out.at[pl.ds(i % half * BLOCK, BLOCK)], sems.at[i]
        ).wait()


def pack(loaded, block_counts, seq_order, after):
    swap = [(0, 1), (1, 0)]
    other = lax.ppermute(loaded, "seq", swap)
    other_counts = lax.ppermute(block_counts, "seq", swap)
    own = seq_order.shape[0] // 2
    width = loaded.shape[1]
    rows = own // 2 * BLOCK
    any_spec = pl.BlockSpec(memory_space=pl.ANY)
    whole = pl.BlockSpec((rows, width), lambda i, *_: (0, 0))
    return pl.pallas_call(
        pack_kernel,
        out_shape=[jax.ShapeDtypeStruct((rows, width), loaded.dtype)] * 2,
        grid_spec=pltpu.PrefetchScalarGridSpec(
            num_scalar_prefetch=3,
            grid=(1,),
            in_specs=[any_spec, any_spec, IN_VMEM],
            out_specs=[whole, whole],
            scratch_shapes=[pltpu.SemaphoreType.DMA((own,))],
        ),
        compiler_params=pltpu.CompilerParams(vmem_limit_bytes=8 * MIB),
    )(in_hbm(block_counts), other_counts, in_hbm(seq_order), in_hbm(loaded), other, after)


GATE, UP, DOWN = range(3)


def bring_start(bring, n, sources, targets, sems):
    copies = []
    for i, (which, step) in enumerate(bring):
        rows, cols = targets[i].shape
        source = sources[which]
        if which == DOWN:
            piece = source.at[:, pl.ds(pl.multiple_of(owner_at(step, n) * cols, cols), cols)]
        else:
            piece = source.at[pl.ds(pl.multiple_of(owner_at(step, n) * rows, rows), rows)]
        copies.append(pltpu.make_async_copy(piece, targets[i], sems.at[i]))
        copies[-1].start()
    return copies


def brought(bring, sources, n):
    shapes = []
    for which, _ in bring:
        rows, cols = sources[which].shape
        shape = (rows, cols // n) if which == DOWN else (rows // n, cols)
        shapes.append(pltpu.VMEM(shape, sources[which].dtype))
    return shapes


def fetch_kernel(bring, n, has_after, *refs):
    first = 3 + has_after
    for copy in bring_start(bring, n, refs[:3], refs[first:-1], refs[-1]):
        copy.wait()


def fetch(sources, bring, after=None):
    n = lax.axis_size("tp")
    outs = brought(bring, sources, n)
    any_spec = pl.BlockSpec(memory_space=pl.ANY)
    more = [] if after is None else [after]
    out = pl.pallas_call(
        functools.partial(fetch_kernel, bring, n, len(more)),
        out_shape=outs,
        in_specs=[any_spec] * 3 + [IN_VMEM] * len(more),
        out_specs=[IN_VMEM] * len(outs),
        scratch_shapes=[pltpu.SemaphoreType.DMA((len(bring),))],
        compiler_params=pltpu.CompilerParams(vmem_limit_bytes=MIB),
        cost_estimate=pl.CostEstimate(
            flops=0, bytes_accessed=len(bring) * 4 * MIB, transcendentals=0
        ),
    )(*sources, *more)
    return dict(zip(bring, out))


def stage_kernel(pieces, has_acc, last, bring, n, *refs):
    refs = list(refs)
    if bring:
        sems = refs.pop()
        sources = [refs.pop(0) for _ in range(3)]
        targets = refs[-len(bring) :]
        bring_start(bring, n, sources, targets, sems)
    xs = [refs.pop(0) for _ in range(pieces)]
    weights = [[refs.pop(0) for _ in range(pieces)] for _ in range(2)]
    acc = [refs.pop(0), refs.pop(0)] if has_acc else None

    def columns(start, tile):
        cols = pl.ds(start, tile)
        sums = []
        for k in range(2):
            total = acc[k][:, cols] if has_acc else None
            for x, weight in zip(xs, weights[k]):
                term = jnp.dot(x[...], weight[:, cols], preferred_element_type=F32)
                total = term if total is None else total + term
            sums.append(total)
        if last:
            gate, up = sums
            refs[0][:, cols] = (gate / (1.0 + jnp.exp(-gate)) * up).astype(BF16)
        else:
            refs[0][:, cols] = sums[0]
            refs[1][:, cols] = sums[1]

    lanes = weights[0][0].shape[1] // 128
    if bring:
        count = next(c for c in range(2, lanes + 1) if lanes % c == 0)
        tile = lanes // count * 128
        pl.loop(0, count)(lambda i: columns(pl.multiple_of(i * tile, tile), tile))
    else:
        tile = 256 if lanes % 2 == 0 else 128
        for i in range(lanes * 128 // tile):
            columns(i * tile, tile)
    if bring:
        for i, target in enumerate(targets):
            pltpu.make_async_copy(target, target, sems.at[i]).wait()


def stage(held, sources, xs, steps, acc=(), last=False, bring=()):
    n = lax.axis_size("tp")
    rows, width = xs[0].shape
    hid = sources[GATE].shape[1]
    operands = [*xs, *[held[which, step] for which in (GATE, UP) for step in steps], *acc]
    if last:
        out_shape = [pltpu.VMEM((rows, hid), BF16)]
    else:
        out_shape = [pltpu.VMEM((rows, hid), F32)] * 2
    outs = len(out_shape)
    in_specs = [IN_VMEM] * len(operands)
    scratch = []
    if bring:
        operands = [*sources, *operands]
        in_specs = [pl.BlockSpec(memory_space=pl.ANY)] * 3 + in_specs
        out_shape += brought(bring, sources, n)
        scratch = [pltpu.SemaphoreType.DMA((len(bring),))]
    aliases = {len(operands) - 2: 0, len(operands) - 1: 1} if acc and not last else {}
    out = pl.pallas_call(
        functools.partial(stage_kernel, len(xs), bool(acc), last, bring, n),
        out_shape=out_shape,
        in_specs=in_specs,
        out_specs=[IN_VMEM] * len(out_shape),
        scratch_shapes=scratch,
        input_output_aliases=aliases,
        compiler_params=pltpu.CompilerParams(vmem_limit_bytes=4 * MIB),
        cost_estimate=pl.CostEstimate(
            flops=12 * rows * width * len(xs) * hid, bytes_accessed=0, transcendentals=0
        ),
    )(*operands)
    held.update(zip(bring, out[outs:]))
    return out[:outs]


def down_kernel(count, h, weight, *refs):
    total = jnp.dot(h[...], weight[...], preferred_element_type=F32)
    for other in refs[:count]:
        total = total + other[...].astype(F32)
    refs[-1][...] = total.astype(refs[-1].dtype)


def down(h, weight, *arrived, dtype=BF16, after=()):
    operands = [h, weight, *arrived, *after]
    return pl.pallas_call(
        functools.partial(down_kernel, len(arrived)),
        out_shape=jax.ShapeDtypeStruct((h.shape[0], weight.shape[1]), dtype),
        in_specs=[IN_VMEM] * len(operands),
        out_specs=IN_VMEM,
        compiler_params=pltpu.CompilerParams(vmem_limit_bytes=4 * MIB),
        cost_estimate=pl.CostEstimate(
            flops=6 * h.size * weight.shape[1], bytes_accessed=0, transcendentals=0
        ),
    )(*operands)


def finish_kernel(own_a, own_b, a_f, a_b, b_f, b_b, out):
    half = own_a.shape[0]
    for i, (own, f, b) in enumerate(((own_a, a_f, a_b), (own_b, b_f, b_b))):
        total = own[...] + f[...].astype(F32) + b[...].astype(F32)
        out[i * half : (i + 1) * half, :] = total.astype(BF16)


def finish(own_a, own_b, arrived_a, arrived_b):
    rows, width = own_a.shape
    return pl.pallas_call(
        finish_kernel,
        out_shape=jax.ShapeDtypeStruct((2 * rows, width), BF16),
        in_specs=[IN_VMEM] * 6,
        out_specs=IN_VMEM,
        compiler_params=pltpu.CompilerParams(vmem_limit_bytes=8 * MIB),
    )(own_a, own_b, *arrived_a, *arrived_b)


def join_kernel(term, arrived, out):
    out[...] = (term[...] + arrived[...].astype(F32)).astype(BF16)


def join(term, arrived):
    return pl.pallas_call(
        join_kernel,
        out_shape=jax.ShapeDtypeStruct(term.shape, BF16),
        in_specs=[IN_VMEM] * 2,
        out_specs=IN_VMEM,
        compiler_params=pltpu.CompilerParams(vmem_limit_bytes=4 * MIB),
        cost_estimate=pl.CostEstimate(flops=0, bytes_accessed=0, transcendentals=0),
    )(term, arrived)


def pair_kernel(h, *refs):
    for weight, out in zip(refs[:2], refs[2:]):
        out[...] = jnp.dot(h[...], weight[...], preferred_element_type=F32).astype(BF16)


def down_pair(h, *weights):
    width = weights[0].shape[1]
    return pl.pallas_call(
        pair_kernel,
        out_shape=[jax.ShapeDtypeStruct((h.shape[0], width), BF16)] * 2,
        in_specs=[IN_VMEM] * 3,
        out_specs=[IN_VMEM] * 2,
        compiler_params=pltpu.CompilerParams(vmem_limit_bytes=4 * MIB),
        cost_estimate=pl.CostEstimate(
            flops=12 * h.size * width, bytes_accessed=0, transcendentals=0
        ),
    )(h, *weights)


def both(*steps):
    return tuple((which, step) for step in steps for which in (GATE, UP))


def body(loaded, block_counts, seq_order, gate_weight, up_weight, down_weight):
    n = lax.axis_size("tp")
    order = ring_order(n)
    fwd, bwd = shift(order, 1), shift(order, -1)
    far = n // 2
    sources = [in_hbm(w) for w in (gate_weight, up_weight, down_weight)]

    later = [slot for step in range(3, far) for slot in both(step, -step)] + list(both(far))
    later += [(DOWN, far)]
    for step in range(far - 1, 0, -1):
        later += [(DOWN, step), (DOWN, -step)]
    later += [(DOWN, 0)]
    stages = 2 * (far - 1)
    shares = [
        tuple(later[i * len(later) // stages : (i + 1) * len(later) // stages])
        for i in range(stages)
    ]

    held = fetch(sources, both(0))
    own_a, own_b = pack(loaded, block_counts, seq_order, held[GATE, 0])
    run = functools.partial(stage, held, sources)

    a_f = a_b = own_a
    b_f = b_b = own_b
    acc_a = run([own_a], [0], bring=both(1))
    acc_b = run([own_b], [0], bring=both(-1))
    held |= fetch(sources, both(2, -2), acc_b[0])
    for step in range(1, far):
        a_f = lax.ppermute(a_f, "tp", fwd)
        a_b = lax.ppermute(a_b, "tp", bwd)
        b_f = lax.ppermute(b_f, "tp", fwd)
        b_b = lax.ppermute(b_b, "tp", bwd)
        acc_a = run([a_f, a_b], [-step, step], acc_a, bring=shares[2 * step - 2])
        acc_b = run([b_f, b_b], [-step, step], acc_b, bring=shares[2 * step - 1])
    a_f = lax.ppermute(a_f, "tp", fwd)
    b_b = lax.ppermute(b_b, "tp", bwd)
    (h_a,) = run([a_f], [far], acc_a, last=True)
    (h_b,) = run([b_b], [far], acc_b, last=True)

    def hop(h, step, sent, way, start):
        arrived = lax.ppermute(sent, "tp", way)
        weight = held[DOWN, step]
        if start:
            return down(h, weight, arrived)
        return join(down(h, weight, dtype=F32, after=[sent]), arrived)

    a_f, a_b = down_pair(h_a, held[DOWN, far], held[DOWN, 1 - far])
    b_b, b_f = down_pair(h_b, held[DOWN, far], held[DOWN, far - 1])
    for step in range(far - 1, 0, -1):
        start = step == far - 1
        a_f = hop(h_a, step, a_f, fwd, start)
        b_b = hop(h_b, -step, b_b, bwd, start)
        if step > 1:
            a_b = hop(h_a, 1 - step, a_b, bwd, start)
            b_f = hop(h_b, step - 1, b_f, fwd, start)
    last = held[DOWN, 0]
    own = down(h_a, last, dtype=F32, after=[a_b]), down(h_b, last, dtype=F32, after=[b_f])
    return finish(
        *own,
        (lax.ppermute(a_f, "tp", fwd), lax.ppermute(a_b, "tp", bwd)),
        (lax.ppermute(b_f, "tp", fwd), lax.ppermute(b_b, "tp", bwd)),
    )


def solution(mesh):
    return jax.shard_map(
        body,
        mesh=mesh,
        in_specs=(
            P(("groups", "seq"), "tp"),
            P(("groups", "seq")),
            P("groups"),
            P(None, "tp"),
            P(None, "tp"),
            P("tp", None),
        ),
        out_specs=P(("groups", "seq"), "tp"),
        check_vma=False,
    )
```
